32 devices in a mesh: ctx: 32 (over z, y, x, core), head: 1.
Axes of the slice: x: 2, y: 2, z: 4, core: 2. Of those that a mesh axis runs over, the one named last changes fastest.
Arguments:
- queries: bfloat16 [1, 12288, 128], P('head', 'ctx'), may hold values from -150 to 150
- keys: bfloat16 [1, 12288, 128], P('head', 'ctx'), may hold values from -8 to 8
- values: bfloat16 [1, 12288, 128], P('head', 'ctx'), may hold values from -6 to 6
- out_weight: bfloat16 [1, 128, 4096], P('head'), may hold values from -0.5 to 0.5
Outputs:
- projected: bfloat16 [12288, 4096], P('ctx', 'head')
The draws below stay inside these ranges and needn't reach their ends.
All inputs are finite; a program needn't handle non-finite values.
Results may differ from the reference program's by a relative error of at most 0.012.
Values may be sent and summed in bfloat16 or wider, within the bound.
No kernel may reach another device: no remote copies, remote signals or barrier semaphores. Data moves between devices by JAX's collectives and lax.ppermute only.
A program may use at most 256 MiB of HBM per device.

```python
import math
import jax
import jax.numpy as jnp
from jax import lax

D = 4096
HD = 128
HEADS = 1
SEQ = 12288


def shared_rows(key):
    base_rows = jnp.clip(jax.random.normal(jax.random.fold_in(key, 11), (HEADS, SEQ, HD), jnp.float32), -6.0, 6.0)
    return base_rows


def draw_keys(key, part):
    base_rows = shared_rows(key)
    return base_rows.astype(jnp.bfloat16)


def draw_queries(key, part):
    key = jax.random.fold_in(key, 4)
    drawn_rows = 3.0 * jnp.clip(jax.random.normal(key, (HEADS, SEQ, HD), jnp.float32), -6.0, 6.0)
    return drawn_rows.astype(jnp.bfloat16)


def steps_of(own_key, extent, pieces, low, top_value):
    def one(position, blocks):
        draws = jax.random.uniform(jax.random.fold_in(jax.random.fold_in(own_key, 6), position), (blocks,), jnp.float32, low / len(pieces), top_value / len(pieces))
        return jnp.repeat(jnp.exp(draws), extent[position] // blocks).reshape((-1,) + (1,) * (len(extent) - position - 1))

    gain = one(*pieces[0])
    for cut in pieces[1:]:
        gain = gain * one(*cut)
    return gain


def centred(stream_key, shape, scale, limit, cuts=(), kind=jnp.bfloat16):
    array = jax.random.normal(stream_key, shape, jnp.float32) * scale
    if len(cuts) > 0:
        array = steps_of(stream_key, shape, cuts, -0.22, 0.18) * array
    return jnp.clip(array, min=-limit, max=limit).astype(kind)


def setup_inputs(seed: int = 0) -> dict:
    splits = jax.random.split(jax.random.key(seed), 5)
    return {
        "queries": draw_queries(jax.random.fold_in(splits[4], 71), 0),
        "keys": draw_keys(jax.random.fold_in(splits[4], 71), 0),
        "values": centred(splits[2], (HEADS, SEQ, HD), 1.0, 6.0, ((1, 32),)),
        "out_weight": centred(splits[3], (HEADS, HD, D), (HEADS * HD) ** -0.5, 0.5),
    }


big_negative = -1e+30
block_rows = 512

def head_attention(query_rows, key_rows, value_rows):
    scaling = 1.0 / math.sqrt(HD)
    total_rows = query_rows.shape[0]
    block_count = total_rows // block_rows
    offsets = jnp.arange(block_rows, dtype=jnp.int32)

    def one_block(block_index):
        first = (block_index * block_rows).astype(jnp.int32)
        block_queries = lax.dynamic_slice_in_dim(query_rows, first, block_rows, 0)
        query_pos = first + offsets

        def fill(key_block, buffer):
            start_key = (key_block * block_rows).astype(jnp.int32)
            block_keys = lax.dynamic_slice_in_dim(key_rows, start_key, block_rows, 0)
            scores = lax.dot_general(block_queries, block_keys, (((1,), (1,)), ((), ())), preferred_element_type=jnp.float32) * scaling
            key_pos = start_key + offsets
            scores = jnp.where(key_pos[None, :] <= query_pos[:, None], scores, jnp.float32(big_negative))
            return lax.dynamic_update_slice(buffer, scores, (jnp.int32(0), start_key))
        buffer = lax.fori_loop(0, block_index + 1, fill, jnp.full((block_rows, total_rows), big_negative, jnp.float32))
        row_max = lax.optimization_barrier(jnp.max(buffer, axis=1))

        def gather_sums(key_block, carried):
            row_total, summed = carried
            start_key = (key_block * block_rows).astype(jnp.int32)
            scores = lax.dynamic_slice_in_dim(buffer, start_key, block_rows, 1)
            block_values = lax.dynamic_slice_in_dim(value_rows, start_key, block_rows, 0)
            exps = jnp.exp(scores - row_max[:, None])
            row_total = row_total + lax.optimization_barrier(jnp.sum(exps, axis=1))
            summed = summed + jnp.dot(exps.astype(jnp.bfloat16), block_values, preferred_element_type=jnp.float32)
            return (row_total, summed)
        init = (jnp.zeros((block_rows,), jnp.float32), jnp.zeros((block_rows, HD), jnp.float32))
        row_total, summed = lax.fori_loop(0, block_index + 1, gather_sums, init)
        return (summed / row_total[:, None]).astype(jnp.bfloat16)
    blocks = lax.map(one_block, jnp.arange(block_count, dtype=jnp.int32))
    return blocks.reshape(total_rows, HD)

def reference(queries, keys, values, out_weight):
    projected = jnp.zeros((queries.shape[1], out_weight.shape[2]), jnp.float32)
    for head_index in range(queries.shape[0]):
        attention = head_attention(queries[head_index], keys[head_index], values[head_index])
        projected = projected + jnp.dot(attention, out_weight[head_index], preferred_element_type=jnp.float32)
    return projected.astype(jnp.bfloat16)
```

```python
import functools
import math

import jax
import jax.numpy as jnp
from jax import lax
from jax.experimental import pallas as pl
from jax.experimental.pallas import tpu as pltpu
from jax.sharding import PartitionSpec as P

PLANES = 4
STAT_ROWS = 16
LEGS = {"a": 2, "b": 1, "c": 3}
NEGATIVE = -1e30
LOG2E = 1.4426950408889634


def dot_tn(a, b):
    return lax.dot_general(a, b, (((0,), (0,)), ((), ())), preferred_element_type=jnp.float32)


def dot_nt(a, b):
    return lax.dot_general(a, b, (((1,), (1,)), ((), ())), preferred_element_type=jnp.float32)


def advance(q, piece_refs, state, step, place=None):
    rows, width = q.shape
    length = piece_refs[0].shape[1]
    factor = LOG2E / math.sqrt(width)

    def scores_of(j):
        scores = dot_nt(jnp.concatenate([ref[0] for ref in piece_refs[j : j + step]], axis=0), q)
        if place is not None:
            index = lax.broadcasted_iota(jnp.int32, (length, 1), 0)
            key_pos = jnp.concatenate([(place ^ (j + i)) * length + index for i in range(step)], axis=0)
            query_pos = place * length + lax.broadcasted_iota(jnp.int32, (1, rows), 1)
            scores = jnp.where(key_pos <= query_pos, scores, NEGATIVE)
        return scores

    coming = scores_of(0)
    for j in range(0, len(piece_refs), step):
        scores = coming
        if j + step < len(piece_refs):
            coming = scores_of(j + step)
        v = jnp.concatenate([ref[1] for ref in piece_refs[j : j + step]], axis=0)
        top = jnp.max(scores, axis=0, keepdims=True)
        if state is not None:
            top = jnp.maximum(top, state[0])
        weights = jnp.exp2((scores - top) * factor)
        total = jnp.sum(weights, axis=0, keepdims=True)
        summed = dot_tn(v, weights.astype(jnp.bfloat16))
        if state is not None:
            kept = jnp.exp2((state[0] - top) * factor)
            total, summed = total + state[1] * kept, summed + state[2] * kept
        state = top, total, summed
    return state


def finish(state, width):
    top, total, summed = state
    return summed / total, top * (LOG2E / math.sqrt(width)) + jnp.log2(total)


def where_earlier(leg, group, body):
    plane = lax.axis_index("ctx") // group
    pl.when((plane ^ leg) > plane)(body)


def store_partial(out_ref, state, width):
    store_partial_of(out_ref, *finish(state, width), width)


def store_partial_of(out_ref, out, lse, width):
    out_ref[:width, :] = out.astype(jnp.bfloat16)
    high = lse.astype(jnp.bfloat16).astype(jnp.float32)
    middle = (lse - high).astype(jnp.bfloat16).astype(jnp.float32)
    low = lse - high - middle
    row = lax.broadcasted_iota(jnp.int32, (STAT_ROWS, 1), 0)
    stat = jnp.where(row == 0, high, jnp.where(row == 1, middle, jnp.where(row == 2, low, 0.0)))
    out_ref[width:, :] = stat.astype(jnp.bfloat16)


def remote_kernel(leg, group, q_ref, *refs):
    piece_refs, out_ref = refs[:-1], refs[-1]
    where_earlier(leg, group, lambda: store_partial(out_ref, advance(q_ref[...], piece_refs, None, 2), q_ref.shape[1]))


def load_partial(ref, width):
    stat = ref[width:, :].astype(jnp.float32)
    row = lax.broadcasted_iota(jnp.int32, (STAT_ROWS, 1), 0)
    return ref[:width, :].astype(jnp.float32), jnp.sum(jnp.where(row < 3, stat, 0.0), axis=0, keepdims=True)


def crossing_kernel(group, q_ref, *refs):
    piece_refs, out_ref = refs[:-1], refs[-1]
    width = q_ref.shape[1]

    def body():
        top, total, summed = advance(q_ref[...], piece_refs, None, 2)
        row = lax.broadcasted_iota(jnp.int32, (8, 1), 0)
        out_ref[:width, :] = summed
        out_ref[width:, :] = jnp.where(row == 0, top, total)

    where_earlier(LEGS["c"], group, body)


def join_kernel(group, state_ref, other_ref, out_ref):
    width = state_ref.shape[0] - 8

    def body():
        state = state_ref[width : width + 1, :], state_ref[width + 1 : width + 2, :], state_ref[:width, :]
        out, lse = finish(state, width)
        other_out, other_lse = load_partial(other_ref, width)
        top = jnp.maximum(lse, other_lse)
        share, other_share = jnp.exp2(lse - top), jnp.exp2(other_lse - top)
        store_partial_of(out_ref, *merged([out, other_out], [share, other_share], top), width)

    where_earlier(LEGS["c"], group, body)


def merged(parts, shares, top):
    total = functools.reduce(jnp.add, shares)
    summed = functools.reduce(jnp.add, [part * (share / total) for part, share in zip(parts, shares)])
    return summed, top + jnp.log2(total)


def own_kernel(group, q_ref, *refs):
    piece_refs, out_ref, lse_ref = refs[:-2], refs[-2], refs[-1]
    place = lax.rem(lax.axis_index("ctx"), group)
    out, lse = finish(advance(q_ref[...], piece_refs, None, 2, place), q_ref.shape[1])
    out_ref[...] = out
    lse_ref[...] = jnp.broadcast_to(lse, lse_ref.shape)


def merge_kernel(group, own_ref, lse_ref, c_ref, b_ref, w_ref, out_ref, attention_ref, tiles_ref, sems):
    width, rows = own_ref.shape
    plane = lax.axis_index("ctx") // group
    lses, parts = [lse_ref[:1, :]], [own_ref[...]]
    for leg, ref in (("c", c_ref), ("b", b_ref)):
        arrived = (plane ^ LEGS[leg]) < plane
        out, lse = load_partial(ref, width)
        lses.append(jnp.where(arrived, lse, NEGATIVE))
        parts.append(jnp.where(arrived, out, 0.0))
    top = functools.reduce(jnp.maximum, lses)
    attention, _ = merged(parts, [jnp.exp2(lse - top) for lse in lses], top)
    attention_ref[...] = jnp.transpose(attention).astype(jnp.bfloat16)
    copies = []
    block = tiles_ref.shape[2]
    for index in range(tiles_ref.shape[0]):
        for at in range(0, block, 256):
            columns = slice(index * block + at, index * block + at + 256)
            tiles_ref[index, :, at : at + 256] = jnp.dot(
                attention_ref[...], w_ref[:, columns], preferred_element_type=jnp.float32
            ).astype(jnp.bfloat16)
        columns = slice(index * block, (index + 1) * block)
        copies.append(pltpu.make_async_copy(tiles_ref.at[index], out_ref.at[:, columns], sems.at[index]))
        copies[-1].start()
    for copy in copies:
        copy.wait()


VMEM = pl.BlockSpec(memory_space=pltpu.VMEM)


def per_device(queries, keys, values, out_weight):
    count = lax.axis_size("ctx")
    group = count // PLANES
    own = queries[0]
    rows, width = own.shape
    columns = out_weight.shape[2]
    key_count = rows * group
    params = pltpu.CompilerParams(vmem_limit_bytes=24 * 1024 * 1024)
    cost = pl.CostEstimate(flops=4 * rows * key_count * width, bytes_accessed=4 * key_count * width, transcendentals=rows * key_count)

    def below(array):
        return lax.ppermute(
            array, "ctx", [(i, i ^ group if i < 2 * group else i ^ 1) for i in range(count)]
        )

    def across(mask, array):
        return lax.ppermute(array, "ctx", [(i, i ^ mask) for i in range(count)])

    k, v, _ = lax.optimization_barrier((keys[0], values[0], own))
    stacked = jnp.stack([k, v])
    pieces = {0: stacked}
    far = group - 2
    held, held_own = stacked, own
    from_two = across(2 * group, own)
    pieces[far] = across(far, stacked)
    pieces[1] = across(1, stacked)
    held, held_own, pieces[1] = lax.optimization_barrier((stacked, own, pieces[1]))
    for mask in range(far - 2, 0, -2):
        pieces[mask] = across(mask, held)
    from_one = across(group, held_own)
    passed = below(from_two)
    waits = {6: from_two, 4: from_one}
    for mask in range(2, group, 2):
        if mask in waits:
            pieces[mask], _ = lax.optimization_barrier((pieces[mask], waits[mask]))
        pieces[mask + 1] = across(1, pieces[mask])
    pieces = [pieces[j] for j in range(group)]

    partial = jax.ShapeDtypeStruct((width + STAT_ROWS, rows), jnp.bfloat16)

    def on_vmem(kernel, shape, count, name, cost):
        return pl.pallas_call(
            kernel,
            out_shape=shape,
            in_specs=[VMEM] * count,
            out_specs=VMEM,
            compiler_params=params,
            cost_estimate=cost,
            name=name,
        )

    small = pl.CostEstimate(flops=rows * width, bytes_accessed=rows * width, transcendentals=0)
    part_a = on_vmem(functools.partial(remote_kernel, LEGS["a"], group), partial, 1 + group, "remote_a", cost)(
        from_two, *pieces
    )
    swapped = below(part_a)
    state_c = on_vmem(
        functools.partial(crossing_kernel, group),
        jax.ShapeDtypeStruct((width + 8, rows), jnp.float32),
        1 + group,
        "remote_c",
        cost,
    )(passed, *pieces)
    joined = on_vmem(functools.partial(join_kernel, group), partial, 2, "join", small)(state_c, swapped)
    step = LEGS["c"] * group
    received_c = lax.ppermute(joined, "ctx", [(i, i ^ step) for i in range(2 * group)])
    part_b = on_vmem(functools.partial(remote_kernel, LEGS["b"], group), partial, 1 + group, "remote_b", cost)(
        from_one, *pieces
    )
    received_b = across(LEGS["b"] * group, part_b)

    own_part, own_lse = pl.pallas_call(
        functools.partial(own_kernel, group),
        out_shape=[jax.ShapeDtypeStruct((height, rows), jnp.float32) for height in (width, 8)],
        in_specs=[VMEM] * (1 + group),
        out_specs=[VMEM, VMEM],
        compiler_params=params,
        cost_estimate=cost,
        name="own",
    )(own, *pieces)

    partial_out = pl.pallas_call(
        functools.partial(merge_kernel, group),
        out_shape=jax.ShapeDtypeStruct((rows, columns), jnp.bfloat16),
        in_specs=[VMEM] * 5,
        out_specs=pl.BlockSpec(memory_space=pl.ANY),
        scratch_shapes=[
            pltpu.VMEM((rows, width), jnp.bfloat16),
            pltpu.VMEM((8, rows, columns // 8), jnp.bfloat16),
            pltpu.SemaphoreType.DMA((8,)),
        ],
        compiler_params=params,
        cost_estimate=pl.CostEstimate(
            flops=2 * rows * width * columns, bytes_accessed=2 * (rows + width) * columns, transcendentals=0
        ),
        name="merge",
    )(own_part, own_lse, received_c, received_b, out_weight[0])
    return lax.psum_scatter(partial_out, "head", scatter_dimension=1, tiled=True)


def solution(mesh):
    placed = (
        P("head", "ctx", None),
        P("head", "ctx", None),
        P("head", "ctx", None),
        P("head", None, None),
    )
    return jax.shard_map(
        per_device, mesh=mesh, in_specs=placed, out_specs=P("ctx", "head"), check_vma=False
    )
```
